256 devices in a mesh: replica: 32 (over y, z), fsdp: 8 (over x, core).
Axes of the slice: x: 4, y: 4, z: 8, core: 2. Of those that a mesh axis runs over, the one named last changes fastest.
Arguments:
- outer_param: float32 [512, 8192], P('fsdp'), may hold values from -4 to 4
- momentum: float32 [512, 8192], P('fsdp'), may hold values from -3 to 3
- inner_weights: bfloat16 [32, 512, 8192], P('replica', 'fsdp'), may hold values from -80 to 80
Outputs:
- new_outer: float32 [512, 8192], P('fsdp')
- new_momentum: float32 [512, 8192], P('fsdp')
- merged: bfloat16 [32, 512, 8192], P('replica', 'fsdp')
The draws below stay inside these ranges and needn't reach their ends.
All inputs are finite; a program needn't handle non-finite values.
Results may differ from the reference program's by a relative error of at most 0.001.
Values sent between devices are 32-bit elements; how exact they have to be, the bound alone decides.
A program may use at most 64 MiB of HBM per device.

```python
import math
import jax
import jax.numpy as jnp
from jax import lax

COLS = 8192
ROWS = 512
N_REPLICA = 32


def shared_parts(key):
    first, second, third, fourth, fifth = jax.random.split(key, 5)
    outer = jnp.clip(jax.random.normal(first, (ROWS, COLS), jnp.float32), -4.0, 4.0)
    trend = 3.0 ** (jnp.arange(ROWS, dtype=jnp.float32) / ROWS)
    row_scale = jnp.exp(jax.random.uniform(second, (ROWS, 1), jnp.float32, 0.0, math.log(10.0))) * trend[:, None]
    col_scale = jnp.exp(jax.random.uniform(third, (1, COLS), jnp.float32, 0.0, math.log(10.0)))
    magnitude = jax.random.uniform(fourth, (ROWS, COLS), jnp.float32, 1.0, 2.0)
    common = jnp.where(jax.random.bernoulli(fifth, 0.5, (ROWS, COLS)), magnitude, -magnitude)
    return (outer, 0.05 * row_scale * col_scale, common)


def draw_outer_param(key, part):
    outer, scale, common = shared_parts(key)
    return outer


def draw_inner_weights(key, part):
    outer, scale, common = shared_parts(key)
    key = jax.random.fold_in(key, 7)
    own = jnp.clip(jax.random.normal(key, (N_REPLICA, ROWS, COLS), jnp.float32), -3.0, 3.0)
    inner = outer[None] - scale[None] * (common[None] + own)
    return inner.astype(jnp.bfloat16)


def block_scale(key, dims, cuts, smallest, high):
    level = 1.0
    for dim, shards_of in cuts:
        draws = jax.random.uniform(jax.random.fold_in(jax.random.fold_in(key, 6), dim), (shards_of,), jnp.float32, smallest / len(cuts), high / len(cuts))
        level = level * jnp.repeat(jnp.exp(draws), dims[dim] // shards_of).reshape((-1,) + (1,) * (len(dims) - 1 - dim))
    return level


def bell_draw(rng, dims, width, reach, shards=(), kind=jnp.bfloat16):
    result = jax.random.normal(rng, dims, jnp.float32) * width
    if len(shards) > 0:
        result = block_scale(rng, dims, shards, -0.22, 0.18) * result
    return jnp.clip(result, min=-reach, max=reach).astype(kind)


def setup_inputs(seed: int = 0) -> dict:
    key_list = jax.random.split(jax.random.key(seed), 4)
    return {
        "outer_param": draw_outer_param(jax.random.fold_in(key_list[3], 71), 0),
        "momentum": bell_draw(key_list[1], (ROWS, COLS), 0.5, 3.0, ((0, 8),), jnp.float32),
        "inner_weights": draw_inner_weights(jax.random.fold_in(key_list[3], 71), 0),
    }


def reference(outer_param, momentum, inner_weights):

    def add_one(total, layer):
        return (total + (outer_param - layer.astype(jnp.float32)), None)
    total, unused = lax.scan(add_one, jnp.zeros_like(outer_param), inner_weights)
    pseudo = total / N_REPLICA
    mean_sq = jnp.sum(pseudo * pseudo) / (ROWS * COLS)
    factor = jnp.minimum(1.0, 0.5 / jnp.sqrt(mean_sq + 1e-06))
    grad = factor * pseudo
    new_momentum = 0.9 * momentum + grad
    new_outer = outer_param - 0.7 * (grad + 0.9 * new_momentum)

    def blend(layer):
        return (0.5 * layer.astype(jnp.float32) + 0.5 * new_outer).astype(jnp.bfloat16)
    merged = lax.map(blend, inner_weights)
    return (new_outer, new_momentum, merged)
```

```python
import jax
import jax.numpy as jnp
from jax import lax
from jax.experimental import pallas as pl
from jax.experimental.pallas import tpu as pltpu
from jax.sharding import PartitionSpec as P

MESH = pl.DeviceIdType.MESH
NY, NZ, NF = 4, 8, 8
ROWS, COLS = 64, 8192
REPLICAS = 32
ENTRIES = 512 * 8192
FLOWS = (
    ("zy", 0, 3072, 3, 1),
    ("yz", 3072, 5120, 2, 2),
)
MAX_COPIES = 128
FROM_Z = {1: 0, -1: 1, 2: 2, -2: 3}
FROM_Y = {1: 4, -1: 5, 2: 6}
PLANES = 7
PEERS = (
    [(0, d, 0, 0) for d in range(1, NZ)] + [(d, 0, 0, 0) for d in range(1, NY)] + [(0, 0, d, 0) for d in range(1, 4)] + [(0, 0, 0, 1)]
)


class AllReduce:
    def __init__(self, acc, got, full, send_sems, recv_sems):
        self.acc, self.got, self.full = acc, got, full
        self.send_sems, self.recv_sems = send_sems, recv_sems
        r, f = lax.axis_index("replica"), lax.axis_index("fsdp")
        self.y, self.z = r // NZ, r % NZ
        self.x, self.c = f // 2, f % 2
        self.sent = []
        self.squares = []

    def device(self, dy=0, dz=0, dx=0, dc=0):
        y, z, x, c = self.y, self.z, self.x, self.c
        y = lax.rem(y + (dy % NY), NY) if dy else y
        z = lax.rem(z + (dz % NZ), NZ) if dz else z
        x = lax.rem(x + (dx % 4), 4) if dx else x
        c = 1 - c if dc else c
        return (y * NZ + z, x * 2 + c)

    def copy(self, src, dst, to):
        i = len(self.sent)
        assert i < MAX_COPIES
        c = pltpu.make_async_remote_copy(
            src_ref=src, dst_ref=dst, send_sem=self.send_sems.at[i], recv_sem=self.recv_sems.at[i],
            device_id=to, device_id_type=MESH)
        c.start()
        self.sent.append(c)
        return c

    @staticmethod
    def at(region):
        r, n, c, w = region
        return (pl.ds(r, n), pl.ds(c, w))

    def push(self, region, to, plane):
        rs, cs = self.at(region)
        return self.copy(self.acc.at[rs, cs], self.got.at[plane, rs, cs], to)

    def pass_on(self, region, to):
        rs, cs = self.at(region)
        return self.copy(self.full.at[rs, cs], self.full.at[rs, cs], to)

    def add(self, region, planes):
        rs, cs = self.at(region)
        total = self.acc[rs, cs]
        for p in planes:
            total = total + self.got[p, rs, cs]
        self.acc[rs, cs] = total

    def shard(self, d, c, w):
        g = lax.rem(self.z + (d % NZ), NZ) if d % NZ else self.z
        return (pl.multiple_of(g * 8, 8), 8, c, w)

    def half_shard(self, d, c, w, s):
        h = w // 2
        return self.shard(d, c if s > 0 else c + h, h)

    def scatter_z(self, c, w, depth):
        sh = lambda d: self.shard(d, c, w)
        z = lambda d: self.device(dz=d)
        both = (1, -1)
        if depth == 4:
            m = {s: self.push(self.half_shard(4, c, w, s), z(s), FROM_Z[s]) for s in both}
            yield
            for s in both:
                m[s].wait_recv()
                self.add(self.half_shard(3 * s, c, w, s), [FROM_Z[s]])
                m[s] = self.push(sh(3 * s), z(s), FROM_Z[s])
            yield
            for s in both:
                m[s].wait_recv()
                self.add(sh(2 * s), [FROM_Z[s]])
                m[s] = self.push(sh(2 * s), z(s), FROM_Z[s])
            yield
        else:
            far = {s: self.push(self.half_shard(4, c, w, s), z(2 * s), FROM_Z[2 * s]) for s in both}
            m = {s: self.push(sh(3 * s), z(s), FROM_Z[s]) for s in both}
            if depth == 2:
                near = {s: self.push(sh(s), z(s), FROM_Z[s]) for s in both}
            yield
            for s in both:
                m[s].wait_recv()
                self.add(sh(2 * s), [FROM_Z[s]])
                far[s].wait_recv()
                self.add(self.half_shard(2 * s, c, w, s), [FROM_Z[2 * s]])
                if depth == 3:
                    m[s] = self.push(sh(2 * s), z(s), FROM_Z[s])
                else:
                    far[s] = self.push(sh(2 * s), z(2 * s), FROM_Z[2 * s])
            yield
            if depth == 2:
                for s in both:
                    near[s].wait_recv()
                    far[s].wait_recv()
                self.add(sh(0), [FROM_Z[d] for d in (1, -1, 2, -2)])
                return
        for s in both:
            m[s].wait_recv()
            self.add(sh(s), [FROM_Z[s]])
            m[s] = self.push(sh(s), z(s), FROM_Z[s])
        yield
        for s in both:
            m[s].wait_recv()
        self.add(sh(0), [FROM_Z[1], FROM_Z[-1]])

    def gather_z(self, c, w, depth):
        sh = lambda d: self.shard(d, c, w)
        z = lambda d: self.device(dz=d)
        both = (1, -1)
        if depth == 2:
            far = {s: self.pass_on(sh(0), z(2 * s)) for s in both}
            near = {s: self.pass_on(sh(0), z(s)) for s in both}
            yield
            for s in both:
                far[s].wait_recv()
                far[s] = self.pass_on(self.half_shard(-2 * s, c, w, s), z(2 * s))
                near[s, 2] = self.pass_on(sh(-2 * s), z(s))
            yield
            for m in (near, far):
                for v in m.values():
                    v.wait_recv()
            return
        m = {s: self.pass_on(sh(0), z(s)) for s in both}
        yield
        for s in both:
            m[s].wait_recv()
            m[s] = self.pass_on(sh(-s), z(s))
        yield
        far = {}
        for s in both:
            m[s].wait_recv()
            if depth == 3:
                far[s] = self.pass_on(self.half_shard(-2 * s, c, w, s), z(2 * s))
            m[s] = self.pass_on(sh(-2 * s), z(s))
        yield
        for s in both:
            m[s].wait_recv()
            if depth == 4:
                far[s] = self.pass_on(self.half_shard(-3 * s, c, w, s), z(s))
        if depth == 4:
            yield
        for s in both:
            far[s].wait_recv()

    def quarter(self, d, r, n, c, w):
        q = lax.rem(self.y + (d % NY), NY) if d % NY else self.y
        return (r, n, pl.multiple_of(c + q * (w // 4), 128), w // 4)

    def half_quarter(self, d, r, n, c, w, s):
        r, n, c, w = self.quarter(d, r, n, c, w)
        if n > 8:
            return (r if s > 0 else r + n // 2, n // 2, c, w)
        return (r, n, c if s > 0 else pl.multiple_of(c + w // 2, 128), w // 2)

    def scatter_y(self, r, n, c, w, depth):
        part = lambda d: self.quarter(d, r, n, c, w)
        y = lambda d: self.device(dy=d)
        both = (1, -1)
        if depth == 1:
            ms = [self.push(part(d), y(d), FROM_Y[d]) for d in (2, 1, -1)]
            yield
            for m in ms:
                m.wait_recv()
            self.add(part(0), list(FROM_Y.values()))
            return
        m = {s: self.push(self.half_quarter(2, r, n, c, w, s), y(s), FROM_Y[s]) for s in both}
        yield
        for s in both:
            m[s].wait_recv()
            self.add(self.half_quarter(s, r, n, c, w, s), [FROM_Y[s]])
            m[s] = self.push(part(s), y(s), FROM_Y[s])
        yield
        for s in both:
            m[s].wait_recv()
        self.add(part(0), [FROM_Y[s] for s in both])

    def gather_y(self, r, n, c, w, depth):
        part = lambda d: self.quarter(d, r, n, c, w)
        y = lambda d: self.device(dy=d)
        both = (1, -1)
        if depth == 1:
            ms = [self.pass_on(part(0), y(d)) for d in (2, 1, -1)]
            yield
            for m in ms:
                m.wait_recv()
            return
        m = {s: self.pass_on(part(0), y(s)) for s in both}
        yield
        for s in both:
            m[s].wait_recv()
            m[s] = self.pass_on(self.half_quarter(-s, r, n, c, w, s), y(s))
        yield
        for s in both:
            m[s].wait_recv()

    def flow(self, order, c, w, z_depth, y_depth):
        mine = self.shard(0, *self.quarter(0, 0, 8, c, w)[2:])
        if order == "zy":
            yield from self.scatter_z(c, w, z_depth)
            yield from self.scatter_y(mine[0], 8, c, w, y_depth)
        else:
            yield from self.scatter_y(0, ROWS, c, w, y_depth)
            yield from self.scatter_z(mine[2], w // 4, z_depth)
        rs, cs = self.at(mine)
        pseudo = self.acc[rs, cs] / REPLICAS
        self.full[rs, cs] = pseudo
        self.squares.append(sum(pseudo[:, i:i + 128] * pseudo[:, i:i + 128] for i in range(0, w // 4, 128)))
        if order == "zy":
            yield from self.gather_y(mine[0], 8, c, w, y_depth)
            yield from self.gather_z(c, w, z_depth)
        else:
            yield from self.gather_z(mine[2], w // 4, z_depth)
            yield from self.gather_y(0, ROWS, c, w, y_depth)

    def clip(self, factor, sums, parts):
        while len(self.squares) < len(FLOWS):
            yield
        total = sum(self.squares)
        stages = [
            [dict(dc=1)], [dict(dx=d) for d in (2, 1, 3)], [dict(dy=d) for d in (2, 1, 3)], [dict(dz=d) for d in (4, 3, 5, 2, 6, 1, 7)]]
        n = 0
        for i, stage in enumerate(stages):
            sums[i] = total
            ms = [self.copy(sums.at[i], parts.at[n + j], self.device(**d)) for j, d in enumerate(stage)]
            yield
            for j, m in enumerate(ms):
                m.wait_recv()
                total = total + parts[n + j]
            n += len(stage)
        mean = jnp.full((8, 128), jnp.sum(total)) / ENTRIES
        factor[...] = jnp.minimum(1.0, 0.5 / jnp.sqrt(mean + 1e-6))


def kernel(outer_hbm, inner_hbm, full, factor, outer, inner, acc, got, sums, parts, send_sems, recv_sems, load_sems):
    ar = AllReduce(acc, got, full, send_sems, recv_sems)
    loads = []
    for i, (_, c, w, _, _) in enumerate(FLOWS):
        cs = pl.ds(c, w)
        for j, (src, dst) in enumerate(((outer_hbm, outer), (inner_hbm, inner))):
            loads.append(pltpu.make_async_copy(src.at[:, cs], dst.at[:, cs], load_sems.at[2 * i + j]))
            loads[-1].start()
    barrier = pltpu.get_barrier_semaphore()
    for p in PEERS:
        pl.semaphore_signal(barrier, inc=1, device_id=ar.device(*p), device_id_type=MESH)
    flows = []
    for i, (order, c, w, z_depth, y_depth) in enumerate(FLOWS):
        loads[2 * i].wait()
        loads[2 * i + 1].wait()
        acc[:, pl.ds(c, w)] = outer[:, pl.ds(c, w)] - inner[:, pl.ds(c, w)].astype(jnp.float32)
        if i == 0:
            pl.semaphore_wait(barrier, len(PEERS))
        g = ar.flow(order, c, w, z_depth, y_depth)
        next(g)
        flows.append(g)
    flows.append(ar.clip(factor, sums, parts))
    while flows:
        flows = [g for g in flows if next(g, flows) is None]
    for c in ar.sent:
        c.wait_send()


def all_reduce(outer_param, inner):
    n = 1 + 3 + 3 + 7
    return pl.pallas_call(
        kernel,
        out_shape=(jax.ShapeDtypeStruct((ROWS, COLS), jnp.float32), jax.ShapeDtypeStruct((8, 128), jnp.float32)),
        in_specs=[pl.BlockSpec(memory_space=pl.ANY)] * 2,
        out_specs=(pl.BlockSpec(memory_space=pltpu.VMEM),) * 2,
        scratch_shapes=[
            pltpu.VMEM((ROWS, COLS), jnp.float32),
            pltpu.VMEM((ROWS, COLS), jnp.bfloat16),
            pltpu.VMEM((ROWS, COLS), jnp.float32),
            pltpu.VMEM((PLANES, ROWS, COLS), jnp.float32),
            pltpu.VMEM((4, 8, 128), jnp.float32),
            pltpu.VMEM((n, 8, 128), jnp.float32),
            pltpu.SemaphoreType.DMA((MAX_COPIES,)),
            pltpu.SemaphoreType.DMA((MAX_COPIES,)),
            pltpu.SemaphoreType.DMA((2 * len(FLOWS),)),
        ],
        compiler_params=pltpu.CompilerParams(collective_id=0, has_side_effects=True, vmem_limit_bytes=28 * 2**20),
    )(outer_param, inner)


def body(outer_param, momentum, inner_weights):
    pseudo, factor = all_reduce(outer_param, inner_weights[0])
    grad = factor[0, 0] * pseudo
    new_momentum = 0.9 * momentum + grad
    new_outer = outer_param - 0.7 * (grad + 0.9 * new_momentum)
    merged = (0.5 * inner_weights.astype(jnp.float32) + 0.5 * new_outer[None]).astype(jnp.bfloat16)
    return (new_outer, new_momentum, merged)


def solution(mesh):
    in_specs = (P("fsdp", None), P("fsdp", None), P("replica", "fsdp", None))
    out_specs = (P("fsdp", None), P("fsdp", None), P("replica", "fsdp", None))
    return jax.shard_map(body, mesh=mesh, in_specs=in_specs, out_specs=out_specs, check_vma=False)
```

```python
import jax
import jax.numpy as jnp
from jax import lax
from jax.experimental import pallas as pl
from jax.experimental.pallas import tpu as pltpu
from jax.sharding import PartitionSpec as P

MESH = pl.DeviceIdType.MESH
NY, NZ, NX = 4, 8, 4
ROWS, COLS = 64, 8192
REPLICAS = 32
ENTRIES = 512 * 8192
FLOWS = (
    (0, 1024, "yz", 2, 2, "zy", 2, 1),
    (1024, 2048, "zy", 3, 1, "zy", 2, 2),
    (3072, 1024, "yz", 2, 2, "yz", 3, 1),
    (4096, 1024, "yz", 1, 2, "yz", 3, 1),
    (5120, 2048, "yz", 2, 2, "yz", 3, 1),
    (7168, 1024, "zy", 2, 1, "zy", 2, 1),
)
ORDER = (
    0, 2, 3, 1, 4, 5, 0, 2, 1, 3, 5, 4, 0, 1, 2, 5, 4, 3, 0, 1, 2, 5, 4, 6, 3, 0, 1, 2, 5, 4, 6, 3, 0, 2, 1, 4, 5, 3, 2, 6, 4, 1, 3, 0, 2, 6, 1, 4,
)
MAX_GROUPS = 47
FROM_Y = {1: 0, -1: 1, 2: 2}
FROM_Z = {1: 3, -1: 4, 2: 5, -2: 6, 3: 7, -3: 8, 4: 9}
PLANES = 10
BOTH = (1, -1)
STAGES = (
    [dict(dx=x, dc=c) for x in (2, 1, 3, 0) for c in (1, 0) if x or c],
    [dict(dz=d) for d in (4, 3, 5, 2, 6, 1, 7)],
    [dict(dy=d) for d in (2, 1, 3)],
)
PEERS = [d for stage in STAGES for d in stage]


class Group:
    def __init__(self, sem):
        self.sem = sem
        self.tiles = 0


class AllReduce:
    def __init__(self, acc, got, full, send_sems, recv_sems):
        self.acc, self.got, self.full = acc, got, full
        self.send_sems, self.recv_sems = send_sems, recv_sems
        r, f = lax.axis_index("replica"), lax.axis_index("fsdp")
        self.y, self.z = r // NZ, r % NZ
        self.x, self.c = f // 2, f % 2
        self.groups = 0
        self.sent = [0, 0]
        self.squares = []

    def device(self, dy=0, dz=0, dx=0, dc=0):
        y, z, x, c = self.y, self.z, self.x, self.c
        y = lax.rem(y + (dy % NY), NY) if dy else y
        z = lax.rem(z + (dz % NZ), NZ) if dz else z
        x = lax.rem(x + (dx % NX), NX) if dx else x
        c = 1 - c if dc else c
        return (y * NZ + z, x * 2 + c)

    def group(self):
        assert self.groups < MAX_GROUPS
        self.groups += 1
        return Group(self.groups - 1)

    def copy(self, group, tiles, src, dst, small=0, **to):
        group.tiles += tiles
        self.sent[small] += tiles
        pltpu.make_async_remote_copy(
            src_ref=src, dst_ref=dst, send_sem=self.send_sems.at[small], recv_sem=self.recv_sems.at[group.sem],
            device_id=self.device(**to), device_id_type=MESH).start()

    def bytes_of(self, tiles):
        for p in range(1, PLANES + 1):
            for r in range(1, 9):
                if tiles % (p * r) == 0 and tiles // (p * r) <= COLS // 128:
                    return self.got.at[pl.ds(0, p), pl.ds(0, 8 * r), pl.ds(0, tiles // (p * r) * 128)]
        raise NotImplementedError

    def waiter(self, tiles, small, sem):
        place = self.bytes_of(tiles)
        return pltpu.make_async_remote_copy(
            src_ref=place, dst_ref=place, send_sem=self.send_sems.at[small], recv_sem=self.recv_sems.at[sem],
            device_id=self.device(dc=1), device_id_type=MESH)

    def wait(self, group):
        self.waiter(group.tiles, 0, group.sem).wait_recv()

    def drain(self):
        for small, tiles in enumerate(self.sent):
            self.waiter(tiles, small, 0).wait_send()

    @staticmethod
    def at(region):
        r, n, c, w = region
        return (pl.ds(r, n), pl.ds(c, w))

    def push(self, group, region, plane, **to):
        rs, cs = self.at(region)
        self.copy(group, region[1] * region[3] // 1024, self.acc.at[rs, cs], self.got.at[plane, rs, cs], **to)

    def push_z(self, group, region, d):
        self.push(group, region, FROM_Z[d], dz=d)

    def push_y(self, group, region, d):
        self.push(group, region, FROM_Y[d], dy=d)

    def pass_on(self, group, region, **to):
        rs, cs = self.at(region)
        self.copy(group, region[1] * region[3] // 1024, self.full.at[rs, cs], self.full.at[rs, cs], **to)

    def add(self, region, planes):
        rs, cs = self.at(region)
        total = self.acc[rs, cs]
        for p in planes:
            total = total + self.got[p, rs, cs]
        self.acc[rs, cs] = total

    def finish(self, region):
        rs, cs = self.at(region)
        pseudo = self.acc[rs, cs] / REPLICAS
        self.full[rs, cs] = pseudo
        self.squares.append(sum(pseudo[:, i:i + 128] * pseudo[:, i:i + 128] for i in range(0, region[3], 128)))

    def shard(self, d, c, w):
        g = lax.rem(self.z + (d % NZ), NZ) if d % NZ else self.z
        return (pl.multiple_of(g * 8, 8), 8, c, w)

    def half_shard(self, d, c, w, s):
        h = w // 2
        return self.shard(d, c if s > 0 else c + h, h)

    def scatter_z(self, c, w, depth):
        sh = lambda d: self.shard(d, c, w)
        half = lambda d, s: self.half_shard(d, c, w, s)
        g = self.group()
        if depth == 1:
            for d in (4, 3, -3, 2, -2, 1, -1):
                self.push_z(g, sh(d), d)
            yield g
            self.wait(g)
            self.add(sh(0), list(FROM_Z.values()))
            return
        if depth == 4:
            for s in BOTH:
                self.push_z(g, half(4, s), s)
            yield g
            self.wait(g)
            g = self.group()
            for s in BOTH:
                self.add(half(3 * s, s), [FROM_Z[s]])
                self.push_z(g, sh(3 * s), s)
            yield g
            self.wait(g)
            g = self.group()
            for s in BOTH:
                self.add(sh(2 * s), [FROM_Z[s]])
                self.push_z(g, sh(2 * s), s)
        else:
            for s in BOTH:
                self.push_z(g, half(4, s), 2 * s)
            for s in BOTH:
                self.push_z(g, sh(3 * s), s)
            after = self.group()
            if depth == 2:
                for s in BOTH:
                    self.push_z(after, sh(s), s)
            yield g
            self.wait(g)
            for s in BOTH:
                self.add(sh(2 * s), [FROM_Z[s]])
                self.add(half(2 * s, s), [FROM_Z[2 * s]])
                self.push_z(after, sh(2 * s), s if depth == 3 else 2 * s)
            g = after
            if depth == 2:
                yield g
                self.wait(g)
                self.add(sh(0), [FROM_Z[d] for d in (1, -1, 2, -2)])
                return
        yield g
        self.wait(g)
        g = self.group()
        for s in BOTH:
            self.add(sh(s), [FROM_Z[s]])
            self.push_z(g, sh(s), s)
        yield g
        self.wait(g)
        self.add(sh(0), [FROM_Z[1], FROM_Z[-1]])

    def gather_z(self, c, w, depth):
        sh = lambda d: self.shard(d, c, w)
        half = lambda d, s: self.half_shard(d, c, w, s)
        g = self.group()
        if depth == 1:
            for d in (4, 3, -3, 2, -2, 1, -1):
                self.pass_on(g, sh(0), dz=d)
            yield g
            self.wait(g)
            return
        if depth == 2:
            for s in BOTH:
                self.pass_on(g, sh(0), dz=2 * s)
            last = self.group()
            for s in BOTH:
                self.pass_on(last, sh(0), dz=s)
            yield g
            self.wait(g)
            for s in BOTH:
                self.pass_on(last, half(-2 * s, s), dz=2 * s)
            for s in BOTH:
                self.pass_on(last, sh(-2 * s), dz=s)
            yield last
            self.wait(last)
            return
        for s in BOTH:
            self.pass_on(g, sh(0), dz=s)
        yield g
        self.wait(g)
        g = self.group()
        for s in BOTH:
            self.pass_on(g, sh(-s), dz=s)
        yield g
        self.wait(g)
        g = self.group()
        if depth == 3:
            for s in BOTH:
                self.pass_on(g, half(-2 * s, s), dz=2 * s)
        for s in BOTH:
            self.pass_on(g, sh(-2 * s), dz=s)
        yield g
        self.wait(g)
        if depth == 4:
            g = self.group()
            for s in BOTH:
                self.pass_on(g, half(-3 * s, s), dz=s)
            yield g
            self.wait(g)

    def quarter(self, d, r, n, c, w):
        q = lax.rem(self.y + (d % NY), NY) if d % NY else self.y
        return (r, n, pl.multiple_of(c + q * (w // 4), 128), w // 4)

    def half_quarter(self, d, r, n, c, w, s):
        r, n, c, w = self.quarter(d, r, n, c, w)
        if n > 8:
            return (r if s > 0 else r + n // 2, n // 2, c, w)
        return (r, n, c if s > 0 else pl.multiple_of(c + w // 2, 128), w // 2)

    def scatter_y(self, r, n, c, w, depth):
        part = lambda d: self.quarter(d, r, n, c, w)
        half = lambda d, s: self.half_quarter(d, r, n, c, w, s)
        g = self.group()
        if depth == 1:
            for d in (2, 1, -1):
                self.push_y(g, part(d), d)
            yield g
            self.wait(g)
            self.add(part(0), list(FROM_Y.values()))
            return
        for s in BOTH:
            self.push_y(g, half(2, s), s)
        yield g
        self.wait(g)
        g = self.group()
        for s in BOTH:
            self.add(half(s, s), [FROM_Y[s]])
            self.push_y(g, part(s), s)
        yield g
        self.wait(g)
        self.add(part(0), [FROM_Y[s] for s in BOTH])

    def gather_y(self, r, n, c, w, depth):
        part = lambda d: self.quarter(d, r, n, c, w)
        g = self.group()
        for d in (2, 1, -1) if depth == 1 else BOTH:
            self.pass_on(g, part(0), dy=d)
        yield g
        self.wait(g)
        if depth == 2:
            g = self.group()
            for s in BOTH:
                self.pass_on(g, self.half_quarter(-s, r, n, c, w, s), dy=s)
            yield g
            self.wait(g)

    def flow(self, c, w, scatter, scatter_z, scatter_y, gather, gather_z, gather_y):
        r, n, q, v = self.shard(0, *self.quarter(0, 0, 8, c, w)[2:])
        if scatter == "zy":
            yield from self.scatter_z(c, w, scatter_z)
            yield from self.scatter_y(r, n, c, w, scatter_y)
        else:
            yield from self.scatter_y(0, ROWS, c, w, scatter_y)
            yield from self.scatter_z(q, v, scatter_z)
        self.finish((r, n, q, v))
        if gather == "yz":
            yield from self.gather_y(r, n, c, w, gather_y)
            yield from self.gather_z(c, w, gather_z)
        else:
            yield from self.gather_z(q, v, gather_z)
            yield from self.gather_y(0, ROWS, c, w, gather_y)

    def clip(self, factor, sums, parts):
        while len(self.squares) < len(FLOWS):
            yield None
        total = sum(self.squares)
        n = 0
        for i, stage in enumerate(STAGES):
            sums[i] = total
            g = self.group()
            for j, d in enumerate(stage):
                self.copy(g, 1, sums.at[i], parts.at[n + j], small=1, **d)
            yield g
            self.wait(g)
            total = total + sum(parts[n + j] for j in range(len(stage)))
            n += len(stage)
        mean = jnp.full((8, 128), jnp.sum(total)) / ENTRIES
        factor[...] = jnp.minimum(1.0, 0.5 / jnp.sqrt(mean + 1e-6))


def exchange(outer_hbm, inner_hbm, momentum_hbm, full, factor, outer, inner, momentum, acc, got, sums, parts, send_sems, recv_sems, load_sems):
    ar = AllReduce(acc, got, full, send_sems, recv_sems)
    barrier = pltpu.get_barrier_semaphore()
    for p in PEERS:
        pl.semaphore_signal(barrier, inc=1, device_id=ar.device(**p), device_id_type=MESH)
    loads = []
    for i, (c, w, *_) in enumerate(FLOWS):
        cs = pl.ds(c, w)
        for j, (src, dst) in enumerate(((outer_hbm, outer), (inner_hbm, inner))):
            loads.append(pltpu.make_async_copy(src.at[:, cs], dst.at[:, cs], load_sems.at[2 * i + j]))
            loads[-1].start()
    loads.append(pltpu.make_async_copy(momentum_hbm, momentum, load_sems.at[len(loads)]))
    loads[-1].start()
    flows = []
    for i, (c, w, *plan) in enumerate(FLOWS):
        loads[2 * i].wait()
        loads[2 * i + 1].wait()
        acc[:, pl.ds(c, w)] = outer[:, pl.ds(c, w)] - inner[:, pl.ds(c, w)].astype(jnp.float32)
        if i == 0:
            pl.semaphore_wait(barrier, len(PEERS))
        flows.append(ar.flow(c, w, *plan))
        next(flows[-1])
    flows.append(ar.clip(factor, sums, parts))
    for i in ORDER:
        next(flows[i], None)
    while flows:
        flows = [g for g in flows if next(g, flows) is not flows]
    ar.drain()
    loads[-1].wait()


def all_reduce(outer_param, inner, momentum):
    array = pltpu.VMEM((ROWS, COLS), jnp.float32)
    operands = [pltpu.with_memory_space_constraint(a, pltpu.HBM) for a in (outer_param, inner, momentum)]
    return pl.pallas_call(
        exchange,
        out_shape=(array, pltpu.VMEM((8, 128), jnp.float32), array, pltpu.VMEM((ROWS, COLS), jnp.bfloat16), array),
        in_specs=[pl.BlockSpec(memory_space=pl.ANY)] * 3,
        out_specs=(pl.BlockSpec(memory_space=pltpu.VMEM),) * 5,
        scratch_shapes=[
            pltpu.VMEM((ROWS, COLS), jnp.float32),
            pltpu.VMEM((PLANES, ROWS, COLS), jnp.float32),
            pltpu.VMEM((len(STAGES), 8, 128), jnp.float32),
            pltpu.VMEM((len(PEERS), 8, 128), jnp.float32),
            pltpu.SemaphoreType.DMA((2,)),
            pltpu.SemaphoreType.DMA((MAX_GROUPS,)),
            pltpu.SemaphoreType.DMA((2 * len(FLOWS) + 1,)),
        ],
        compiler_params=pltpu.CompilerParams(collective_id=0, has_side_effects=True, vmem_limit_bytes=32 * 2**20),
    )(*operands)


BLOCK = (16, 4096)
STRIP = 512


def update(pseudo, factor, outer, inner, momentum, new_outer_hbm, new_momentum_hbm, merged_hbm, new_outer, new_momentum, merged, sems):
    f = jnp.broadcast_to(factor[0:1, 0:1], (BLOCK[0], STRIP))
    stores = []
    for r in range(0, ROWS, BLOCK[0]):
        for c in range(0, COLS, BLOCK[1]):
            rs = pl.ds(r, BLOCK[0])

            @pl.loop(c, c + BLOCK[1], step=STRIP)
            def _(i):
                cs = pl.ds(pl.multiple_of(i, STRIP), STRIP)
                grad = f * pseudo[rs, cs]
                m = 0.9 * momentum[rs, cs] + grad
                o = outer[rs, cs] - 0.7 * (grad + 0.9 * m)
                new_momentum[rs, cs] = m
                new_outer[rs, cs] = o
                merged[rs, cs] = (0.5 * inner[rs, cs].astype(jnp.float32) + 0.5 * o).astype(jnp.bfloat16)

            cs = pl.ds(c, BLOCK[1])
            for src, dst in ((new_outer, new_outer_hbm), (new_momentum, new_momentum_hbm), (merged, merged_hbm)):
                stores.append(pltpu.make_async_copy(src.at[rs, cs], dst.at[rs, cs], sems.at[len(stores)]))
                stores[-1].start()
    for s in stores:
        s.wait()


def outer_update(pseudo, factor, outer, inner, momentum):
    shapes = ((ROWS, COLS), jnp.float32), ((ROWS, COLS), jnp.float32), ((ROWS, COLS), jnp.bfloat16)
    return pl.pallas_call(
        update,
        out_shape=[pltpu.HBM(*s) for s in shapes],
        in_specs=[pl.BlockSpec(memory_space=pltpu.VMEM)] * 5,
        out_specs=[pl.BlockSpec(memory_space=pltpu.HBM)] * 3,
        scratch_shapes=[pltpu.VMEM(*s) for s in shapes] + [pltpu.SemaphoreType.DMA((3 * (ROWS // BLOCK[0]) * (COLS // BLOCK[1]),))],
        compiler_params=pltpu.CompilerParams(vmem_limit_bytes=16 * 2**20),
    )(pseudo, factor, outer, inner, momentum)


def body(outer_param, momentum, inner_weights):
    inner = inner_weights[0]
    new_outer, new_momentum, merged = outer_update(*all_reduce(outer_param, inner, momentum))
    return (new_outer, new_momentum, merged[None])


def solution(mesh):
    in_specs = (P("fsdp", None), P("fsdp", None), P("replica", "fsdp", None))
    out_specs = (P("fsdp", None), P("fsdp", None), P("replica", "fsdp", None))
    return jax.shard_map(body, mesh=mesh, in_specs=in_specs, out_specs=out_specs, check_vma=False)
```

```python
import jax
import jax.numpy as jnp
from jax import lax
from jax.experimental import pallas as pl
from jax.experimental.pallas import tpu as pltpu
from jax.sharding import PartitionSpec as P

MESH = pl.DeviceIdType.MESH
NY, NZ, NX = 4, 8, 4
ROWS, COLS = 64, 8192
REPLICAS = 32
ENTRIES = 512 * 8192
FLOWS = (
    (0, 2048, "yz", 2, 2, "yz", 3, 1),
    (2048, 1024, "zy", 3, 1, "zy", 1, 2),
    (3072, 2048, "yz", 2, 2, "yz", 3, 1),
    (5120, 2048, "zy", 3, 1, "zy", 1, 1),
    (7168, 1024, "yz", 2, 2, "zy", 2, 1),
)
ORDER = (
    0, 1, 3, 2, 4, 0, 1, 2, 3, 4, 1, 0, 3, 2, 1, 4, 0, 3, 2, 1, 4, 0, 3, 2, 4, 5, 0, 1, 2, 4, 3, 0, 1, 5, 2, 4, 0, 1, 5, 2, 3, 0, 4, 5, 2,
)
MAX_GROUPS = 39
FROM_Y = {1: 0, -1: 1, 2: 2}
FROM_Z = {1: 3, -1: 4, 2: 5, -2: 6, 3: 7, -3: 8, 4: 9}
SPARE = (5, 6, 7, 8, 9, 10)
PLANES = 11
BOTH = (1, -1)
STAGES = (
    [dict(dz=d) for d in (4, 3, 5, 2, 6, 1, 7)],
    [dict(dx=x, dc=c) for x in (2, 1, 3, 0) for c in (1, 0) if x or c],
    [dict(dy=d) for d in (2, 1, 3)],
)
PEERS = [d for stage in STAGES for d in stage]


CORNERS = sorted({(2 if z == 2 else 1) for _, _, *p in FLOWS for z, y in ((p[1], p[2]), (p[4], p[5])) if y == 0})
PEERS += [dict(dz=s * d, dy=q) for d in CORNERS for s in BOTH for q in (2, 1, -1)]
PEERS.sort(key=lambda p: -sum(min(d % n, -d % n) for d, n in ((p.get("dz", 0), NZ), (p.get("dy", 0), NY), (p.get("dx", 0), NX))))


class Group:
    def __init__(self, sem):
        self.sem = sem
        self.tiles = 0


class AllReduce:
    def __init__(self, acc, got, full, send_sems, recv_sems):
        self.acc, self.got, self.full = acc, got, full
        self.send_sems, self.recv_sems = send_sems, recv_sems
        r, f = lax.axis_index("replica"), lax.axis_index("fsdp")
        y, z, x = r // NZ, r % NZ, f // 2
        self.c = f % 2
        self.ys = [y] + [lax.rem(y + d, NY) for d in range(1, NY)]
        self.zs = [z] + [lax.rem(z + d, NZ) for d in range(1, NZ)]
        self.xs = [x] + [lax.rem(x + d, NX) for d in range(1, NX)]
        self.rows = [pl.multiple_of(g * 8, 8) for g in self.zs]
        self.groups = 0
        self.sent = [0, 0]
        self.squares = []

    def device(self, dy=0, dz=0, dx=0, dc=0):
        c = 1 - self.c if dc else self.c
        return (self.ys[dy % NY] * NZ + self.zs[dz % NZ], self.xs[dx % NX] * 2 + c)

    def group(self):
        assert self.groups < MAX_GROUPS
        self.groups += 1
        return Group(self.groups - 1)

    def copy(self, group, tiles, src, dst, small=0, **to):
        group.tiles += tiles
        self.sent[small] += tiles
        pltpu.make_async_remote_copy(
            src_ref=src, dst_ref=dst, send_sem=self.send_sems.at[small], recv_sem=self.recv_sems.at[group.sem],
            device_id=self.device(**to), device_id_type=MESH).start()

    def bytes_of(self, tiles):
        for p in range(1, PLANES + 1):
            for r in range(1, 9):
                if tiles % (p * r) == 0 and tiles // (p * r) <= COLS // 128:
                    return self.got.at[pl.ds(0, p), pl.ds(0, 8 * r), pl.ds(0, tiles // (p * r) * 128)]
        raise NotImplementedError

    def waiter(self, tiles, small, sem):
        place = self.bytes_of(tiles)
        return pltpu.make_async_remote_copy(
            src_ref=place, dst_ref=place, send_sem=self.send_sems.at[small], recv_sem=self.recv_sems.at[sem],
            device_id=self.device(dc=1), device_id_type=MESH)

    def wait(self, group):
        self.waiter(group.tiles, 0, group.sem).wait_recv()

    def drain(self):
        for small, tiles in enumerate(self.sent):
            self.waiter(tiles, small, 0).wait_send()

    @staticmethod
    def at(region):
        r, n, c, w = region
        return (pl.ds(r, n), pl.ds(c, w))

    def push(self, group, region, plane, **to):
        rs, cs = self.at(region)
        self.copy(group, region[1] * region[3] // 1024, self.acc.at[rs, cs], self.got.at[plane, rs, cs], **to)

    def push_z(self, group, region, d):
        self.push(group, region, FROM_Z[d], dz=d)

    def push_y(self, group, region, d):
        self.push(group, region, FROM_Y[d], dy=d)

    def pass_on(self, group, region, **to):
        rs, cs = self.at(region)
        self.copy(group, region[1] * region[3] // 1024, self.full.at[rs, cs], self.full.at[rs, cs], **to)

    def add(self, region, planes):
        rs, cs = self.at(region)
        total = self.acc[rs, cs]
        for p in planes:
            total = total + self.got[p, rs, cs]
        self.acc[rs, cs] = total

    def finish(self, region):
        rs, cs = self.at(region)
        pseudo = self.acc[rs, cs] / REPLICAS
        self.full[rs, cs] = pseudo
        self.squares.append(sum(pseudo[:, i:i + 128] * pseudo[:, i:i + 128] for i in range(0, region[3], 128)))

    def finish_rows(self, region, mine):
        rs, cs = self.at(region)
        even = self.acc[rs, cs] + self.got[FROM_Y[2], rs, cs]
        odd = self.got[FROM_Y[1], rs, cs] + self.got[FROM_Y[-1], rs, cs]
        self.full[rs, cs] = (even + odd) / REPLICAS
        rs, cs = self.at(mine)
        pseudo = self.full[rs, cs]
        self.squares.append(sum(pseudo[:, i:i + 128] * pseudo[:, i:i + 128] for i in range(0, mine[3], 128)))

    def shard(self, d, c, w):
        return (self.rows[d % NZ], 8, c, w)

    def half_shard(self, d, c, w, s):
        h = w // 2
        return self.shard(d, c if s > 0 else c + h, h)

    def push_corners(self, group, c, w, d):
        for q in (2, 1, -1, 0):
            for s in BOTH:
                plane = FROM_Z[s * d] if q == 0 else SPARE[(1 - s) // 2 * 3 + q % NY - 1]
                self.push(group, self.quarter(q, *self.shard(s * d, c, w)), plane, dz=s * d, dy=q)

    def push_rows(self, group, c, w):
        for q in (2, 1, -1):
            self.push_y(group, self.quarter(q, *self.shard(0, c, w)), q)

    def add_corners(self, c, w, d):
        self.add(self.quarter(0, *self.shard(0, c, w)), [FROM_Z[d], FROM_Z[-d], *SPARE, *FROM_Y.values()])

    def scatter_z(self, c, w, depth, merged=False):
        sh = lambda d: self.shard(d, c, w)
        half = lambda d, s: self.half_shard(d, c, w, s)
        g = self.group()
        if merged and depth == 2:
            for s in BOTH:
                self.push_z(g, half(4, s), 2 * s)
            for s in BOTH:
                self.push_z(g, sh(3 * s), s)
            for s in BOTH:
                self.push_z(g, sh(s), s)
            yield g
            self.wait(g)
            g = self.group()
            for s in BOTH:
                self.add(sh(2 * s), [FROM_Z[s]])
                self.add(half(2 * s, s), [FROM_Z[2 * s]])
            self.push_corners(g, c, w, 2)
            self.add(sh(0), [FROM_Z[s] for s in BOTH])
            self.push_rows(g, c, w)
            yield g
            self.wait(g)
            self.add_corners(c, w, 2)
            return
        if depth == 1:
            for d in (4, 3, -3, 2, -2, 1, -1):
                self.push_z(g, sh(d), d)
            yield g
            self.wait(g)
            self.add(sh(0), list(FROM_Z.values()))
            return
        if depth == 4:
            for s in BOTH:
                self.push_z(g, half(4, s), s)
            yield g
            self.wait(g)
            g = self.group()
            for s in BOTH:
                self.add(half(3 * s, s), [FROM_Z[s]])
                self.push_z(g, sh(3 * s), s)
            yield g
            self.wait(g)
            g = self.group()
            for s in BOTH:
                self.add(sh(2 * s), [FROM_Z[s]])
                self.push_z(g, sh(2 * s), s)
        else:
            for s in BOTH:
                self.push_z(g, half(4, s), 2 * s)
            for s in BOTH:
                self.push_z(g, sh(3 * s), s)
            after = self.group()
            if depth == 2:
                for s in BOTH:
                    self.push_z(after, sh(s), s)
            yield g
            self.wait(g)
            for s in BOTH:
                self.add(sh(2 * s), [FROM_Z[s]])
                self.add(half(2 * s, s), [FROM_Z[2 * s]])
                self.push_z(after, sh(2 * s), s if depth == 3 else 2 * s)
            g = after
            if depth == 2:
                yield g
                self.wait(g)
                self.add(sh(0), [FROM_Z[d] for d in (1, -1, 2, -2)])
                return
        if merged:
            last = self.group()
            self.push_rows(last, c, w)
        yield g
        self.wait(g)
        if merged:
            for s in BOTH:
                self.add(sh(s), [FROM_Z[s]])
            self.push_corners(last, c, w, 1)
            yield last
            self.wait(last)
            self.add_corners(c, w, 1)
            return
        g = self.group()
        for s in BOTH:
            self.add(sh(s), [FROM_Z[s]])
            self.push_z(g, sh(s), s)
        yield g
        self.wait(g)
        self.add(sh(0), [FROM_Z[1], FROM_Z[-1]])

    def gather_z(self, c, w, depth, merged=False):
        sh = lambda d: self.shard(d, c, w)
        half = lambda d, s: self.half_shard(d, c, w, s)
        g = self.group()
        if merged:
            mine = self.quarter(0, *sh(0))
            d = 2 if depth == 2 else 1
            for q in (2, 1, -1, 0):
                for s in BOTH:
                    self.pass_on(g, mine, dz=s * d, dy=q)
                if q:
                    self.pass_on(g, mine, dy=q)
            yield g
            self.wait(g)
            g = self.group()
            if depth == 2:
                for s in BOTH:
                    self.pass_on(g, half(-2 * s, s), dz=2 * s)
                for s in BOTH:
                    self.pass_on(g, sh(0), dz=s)
                    self.pass_on(g, sh(-2 * s), dz=s)
                yield g
                self.wait(g)
                return
            for s in BOTH:
                self.pass_on(g, sh(-s), dz=s)
        if depth == 1:
            for d in (4, 3, -3, 2, -2, 1, -1):
                self.pass_on(g, sh(0), dz=d)
            yield g
            self.wait(g)
            return
        if depth == 2 and not merged:
            for s in BOTH:
                self.pass_on(g, sh(0), dz=2 * s)
            last = self.group()
            for s in BOTH:
                self.pass_on(last, sh(0), dz=s)
            yield g
            self.wait(g)
            for s in BOTH:
                self.pass_on(last, half(-2 * s, s), dz=2 * s)
            for s in BOTH:
                self.pass_on(last, sh(-2 * s), dz=s)
            yield last
            self.wait(last)
            return
        if not merged:
            for s in BOTH:
                self.pass_on(g, sh(0), dz=s)
            yield g
            self.wait(g)
            g = self.group()
            for s in BOTH:
                self.pass_on(g, sh(-s), dz=s)
        yield g
        self.wait(g)
        g = self.group()
        if depth == 3:
            for s in BOTH:
                self.pass_on(g, half(-2 * s, s), dz=2 * s)
        for s in BOTH:
            self.pass_on(g, sh(-2 * s), dz=s)
        yield g
        self.wait(g)
        if depth == 4:
            g = self.group()
            for s in BOTH:
                self.pass_on(g, half(-3 * s, s), dz=s)
            yield g
            self.wait(g)

    def quarter(self, d, r, n, c, w):
        return (r, n, pl.multiple_of(c + self.ys[d % NY] * (w // 4), 128), w // 4)

    def half_quarter(self, d, r, n, c, w, s):
        r, n, c, w = self.quarter(d, r, n, c, w)
        if n > 8:
            return (r if s > 0 else r + n // 2, n // 2, c, w)
        return (r, n, c if s > 0 else pl.multiple_of(c + w // 2, 128), w // 2)

    def scatter_y(self, r, n, c, w, depth):
        part = lambda d: self.quarter(d, r, n, c, w)
        half = lambda d, s: self.half_quarter(d, r, n, c, w, s)
        g = self.group()
        if depth == 1:
            for d in (2, 1, -1):
                self.push_y(g, part(d), d)
            yield g
            self.wait(g)
            self.add(part(0), list(FROM_Y.values()))
            return
        for s in BOTH:
            self.push_y(g, half(2, s), s)
        yield g
        self.wait(g)
        g = self.group()
        for s in BOTH:
            self.add(half(s, s), [FROM_Y[s]])
            self.push_y(g, part(s), s)
        yield g
        self.wait(g)
        self.add(part(0), [FROM_Y[s] for s in BOTH])

    def gather_y(self, r, n, c, w, depth):
        part = lambda d: self.quarter(d, r, n, c, w)
        g = self.group()
        for d in (2, 1, -1) if depth == 1 else BOTH:
            self.pass_on(g, part(0), dy=d)
        yield g
        self.wait(g)
        if depth == 2:
            g = self.group()
            for s in BOTH:
                self.pass_on(g, self.half_quarter(-s, r, n, c, w, s), dy=s)
            yield g
            self.wait(g)

    def flow(self, c, w, scatter, scatter_z, scatter_y, gather, gather_z, gather_y):
        r, n, q, v = self.shard(0, *self.quarter(0, 0, 8, c, w)[2:])
        if scatter == "zy":
            yield from self.scatter_z(c, w, scatter_z, scatter_y == 0)
            if scatter_y == 3:
                g = self.group()
                for d in (2, 1, -1):
                    self.push_y(g, (r, n, c, w), d)
                yield g
                self.wait(g)
            elif scatter_y:
                yield from self.scatter_y(r, n, c, w, scatter_y)
        else:
            yield from self.scatter_y(0, ROWS, c, w, scatter_y)
            yield from self.scatter_z(q, v, scatter_z)
        if scatter_y == 3:
            self.finish_rows((r, n, c, w), (r, n, q, v))
        else:
            self.finish((r, n, q, v))
        if gather == "yz":
            if gather_y in (1, 2):
                yield from self.gather_y(r, n, c, w, gather_y)
            yield from self.gather_z(c, w, gather_z, gather_y == 0)
        else:
            yield from self.gather_z(q, v, gather_z)
            yield from self.gather_y(0, ROWS, c, w, gather_y)

    def clip(self, factor, sums, parts):
        while len(self.squares) < len(FLOWS):
            yield None
        total = sum(self.squares)
        n = 0
        for i, stage in enumerate(STAGES):
            sums[i] = total
            g = self.group()
            for j, d in enumerate(stage):
                self.copy(g, 1, sums.at[i], parts.at[n + j], small=1, **d)
            yield g
            self.wait(g)
            total = total + sum(parts[n + j] for j in range(len(stage)))
            n += len(stage)
        mean = jnp.full((8, 128), jnp.sum(total)) / ENTRIES
        factor[...] = jnp.minimum(1.0, 0.5 / jnp.sqrt(mean + 1e-6))


def exchange(outer_hbm, inner_hbm, momentum_hbm, full, factor, outer, inner, momentum, acc, got, sums, parts, send_sems, recv_sems, load_sems):
    ar = AllReduce(acc, got, full, send_sems, recv_sems)
    barrier = pltpu.get_barrier_semaphore()
    loads = []
    for i, (c, w, *_) in enumerate(FLOWS):
        cs = pl.ds(c, w)
        for j, (src, dst) in enumerate(((outer_hbm, outer), (inner_hbm, inner))):
            loads.append(pltpu.make_async_copy(src.at[:, cs], dst.at[:, cs], load_sems.at[2 * i + j]))
    last_load = pltpu.make_async_copy(momentum_hbm, momentum, load_sems.at[len(loads)])
    starts = list(dict.fromkeys(i for i in ORDER if i < len(FLOWS)))
    for p in PEERS:
        pl.semaphore_signal(barrier, inc=1, device_id=ar.device(**p), device_id_type=MESH)
    for i in starts:
        loads[2 * i].start()
        loads[2 * i + 1].start()

    def flow(i, c, w, *plan):
        loads[2 * i].wait()
        loads[2 * i + 1].wait()
        acc[:, pl.ds(c, w)] = outer[:, pl.ds(c, w)] - inner[:, pl.ds(c, w)].astype(jnp.float32)
        if i == starts[0]:
            pl.semaphore_wait(barrier, len(PEERS))
        yield from ar.flow(c, w, *plan)

    flows = [flow(i, *f) for i, f in enumerate(FLOWS)] + [ar.clip(factor, sums, parts)]
    for n, i in enumerate(ORDER):
        next(flows[i], None)
        if n == 2 * len(FLOWS):
            last_load.start()
    assert all(next(g, flows) is flows for g in flows)
    ar.drain()
    last_load.wait()


def all_reduce(outer_param, inner, momentum):
    array = pltpu.VMEM((ROWS, COLS), jnp.float32)
    operands = [pltpu.with_memory_space_constraint(a, pltpu.HBM) for a in (outer_param, inner, momentum)]
    return pl.pallas_call(
        exchange,
        out_shape=(array, pltpu.VMEM((8, 128), jnp.float32), array, pltpu.VMEM((ROWS, COLS), jnp.bfloat16), array),
        in_specs=[pl.BlockSpec(memory_space=pl.ANY)] * 3,
        out_specs=(pl.BlockSpec(memory_space=pltpu.VMEM),) * 5,
        scratch_shapes=[
            pltpu.VMEM((ROWS, COLS), jnp.float32),
            pltpu.VMEM((PLANES, ROWS, COLS), jnp.float32),
            pltpu.VMEM((len(STAGES), 8, 128), jnp.float32),
            pltpu.VMEM((len(PEERS), 8, 128), jnp.float32),
            pltpu.SemaphoreType.DMA((2,)),
            pltpu.SemaphoreType.DMA((MAX_GROUPS,)),
            pltpu.SemaphoreType.DMA((2 * len(FLOWS) + 1,)),
        ],
        compiler_params=pltpu.CompilerParams(collective_id=0, has_side_effects=True, vmem_limit_bytes=32 * 2**20),
    )(*operands)


BLOCK = (16, 4096)
STRIP = 512


def update(pseudo, factor, outer, inner, momentum, new_outer_hbm, new_momentum_hbm, merged_hbm, new_outer, new_momentum, merged, sems):
    f = jnp.broadcast_to(factor[0:1, 0:1], (BLOCK[0], STRIP))
    stores = []
    for r in range(0, ROWS, BLOCK[0]):
        for c in range(0, COLS, BLOCK[1]):
            rs = pl.ds(r, BLOCK[0])

            @pl.loop(c, c + BLOCK[1], step=STRIP)
            def _(i):
                cs = pl.ds(pl.multiple_of(i, STRIP), STRIP)
                grad = f * pseudo[rs, cs]
                m = 0.9 * momentum[rs, cs] + grad
                o = outer[rs, cs] - 0.7 * (grad + 0.9 * m)
                new_momentum[rs, cs] = m
                new_outer[rs, cs] = o
                merged[rs, cs] = (0.5 * inner[rs, cs].astype(jnp.float32) + 0.5 * o).astype(jnp.bfloat16)

            cs = pl.ds(c, BLOCK[1])
            for src, dst in ((new_outer, new_outer_hbm), (new_momentum, new_momentum_hbm), (merged, merged_hbm)):
                stores.append(pltpu.make_async_copy(src.at[rs, cs], dst.at[rs, cs], sems.at[len(stores)]))
                stores[-1].start()
    for s in stores:
        s.wait()


def outer_update(pseudo, factor, outer, inner, momentum):
    shapes = ((ROWS, COLS), jnp.float32), ((ROWS, COLS), jnp.float32), ((ROWS, COLS), jnp.bfloat16)
    return pl.pallas_call(
        update,
        out_shape=[pltpu.HBM(*s) for s in shapes],
        in_specs=[pl.BlockSpec(memory_space=pltpu.VMEM)] * 5,
        out_specs=[pl.BlockSpec(memory_space=pltpu.HBM)] * 3,
        scratch_shapes=[pltpu.VMEM(*s) for s in shapes] + [pltpu.SemaphoreType.DMA((3 * (ROWS // BLOCK[0]) * (COLS // BLOCK[1]),))],
        compiler_params=pltpu.CompilerParams(vmem_limit_bytes=16 * 2**20),
    )(pseudo, factor, outer, inner, momentum)


def body(outer_param, momentum, inner_weights):
    inner = inner_weights[0]
    new_outer, new_momentum, merged = outer_update(*all_reduce(outer_param, inner, momentum))
    return (new_outer, new_momentum, merged[None])


def solution(mesh):
    in_specs = (P("fsdp", None), P("fsdp", None), P("replica", "fsdp", None))
    out_specs = (P("fsdp", None), P("fsdp", None), P("replica", "fsdp", None))
    return jax.shard_map(body, mesh=mesh, in_specs=in_specs, out_specs=out_specs, check_vma=False)
```

```python
import jax
import jax.numpy as jnp
from jax import lax
from jax.experimental import pallas as pl
from jax.experimental.pallas import tpu as pltpu
from jax.sharding import PartitionSpec as P

MESH = pl.DeviceIdType.MESH
NY, NZ, NX = 4, 8, 4
ROWS, COLS = 64, 8192
REPLICAS = 32
ENTRIES = 512 * 8192
FLOWS = (
    (0, 2048, "yz", 2, 2, "yz", 3, 1),
    (2048, 1024, "zy", 3, 1, "zy", 1, 2),
    (3072, 2048, "yz", 2, 2, "yz", 3, 1),
    (5120, 2048, "zy", 3, 1, "zy", 1, 1),
    (7168, 1024, "yz", 2, 2, "zy", 2, 1),
)
ORDER = (
    0, 1, 3, 2, 4, 0, 1, 2, 3, 4, 1, 0, 3, 2, 1, 4, 0, 3, 2, 1, 4, 0, 3, 2, 4, 5, 0, 1, 2, 4, 3, 0, 1, 5, 2, 4, 0, 1, 5, 2, 3, 0, 4, 5, 2,
)
MAX_GROUPS = 39
FROM_Y = {1: 0, -1: 1, 2: 2}
FROM_Z = {1: 3, -1: 4, 2: 5, -2: 6, 3: 7, -3: 8, 4: 9}
SPARE = (5, 6, 7, 8, 9, 10)
PLANES = 11
BOTH = (1, -1)
STAGES = (
    [dict(dz=d) for d in (4, 3, 5, 2, 6, 1, 7)],
    [dict(dx=x, dc=c) for x in (2, 1, 3, 0) for c in (1, 0) if x or c],
    [dict(dy=d) for d in (2, 1, 3)],
)
PEERS = [d for stage in STAGES for d in stage]


CORNERS = sorted({(2 if z == 2 else 1) for _, _, *p in FLOWS for z, y in ((p[1], p[2]), (p[4], p[5])) if y == 0})
PEERS += [dict(dz=s * d, dy=q) for d in CORNERS for s in BOTH for q in (2, 1, -1)]
PEERS.sort(key=lambda p: -sum(min(d % n, -d % n) for d, n in ((p.get("dz", 0), NZ), (p.get("dy", 0), NY), (p.get("dx", 0), NX))))


class Group:
    def __init__(self, sem):
        self.sem = sem
        self.tiles = 0


class AllReduce:
    def __init__(self, acc, got, full, send_sems, recv_sems):
        self.acc, self.got, self.full = acc, got, full
        self.send_sems, self.recv_sems = send_sems, recv_sems
        r, f = lax.axis_index("replica"), lax.axis_index("fsdp")
        y, z, x = r // NZ, r % NZ, f // 2
        self.c = f % 2
        self.ys = [y] + [lax.rem(y + d, NY) for d in range(1, NY)]
        self.zs = [z] + [lax.rem(z + d, NZ) for d in range(1, NZ)]
        self.xs = [x] + [lax.rem(x + d, NX) for d in range(1, NX)]
        self.rows = [pl.multiple_of(g * 8, 8) for g in self.zs]
        self.groups = 0
        self.sent = [0, 0]
        self.squares = []

    def device(self, dy=0, dz=0, dx=0, dc=0):
        c = 1 - self.c if dc else self.c
        return (self.ys[dy % NY] * NZ + self.zs[dz % NZ], self.xs[dx % NX] * 2 + c)

    def group(self):
        assert self.groups < MAX_GROUPS
        self.groups += 1
        return Group(self.groups - 1)

    def copy(self, group, tiles, src, dst, small=0, **to):
        group.tiles += tiles
        self.sent[small] += tiles
        pltpu.make_async_remote_copy(
            src_ref=src, dst_ref=dst, send_sem=self.send_sems.at[small], recv_sem=self.recv_sems.at[group.sem],
            device_id=self.device(**to), device_id_type=MESH).start()

    def bytes_of(self, tiles):
        for p in range(1, PLANES + 1):
            for r in range(1, 9):
                if tiles % (p * r) == 0 and tiles // (p * r) <= COLS // 128:
                    return self.got.at[pl.ds(0, p), pl.ds(0, 8 * r), pl.ds(0, tiles // (p * r) * 128)]
        raise NotImplementedError

    def waiter(self, tiles, small, sem):
        place = self.bytes_of(tiles)
        return pltpu.make_async_remote_copy(
            src_ref=place, dst_ref=place, send_sem=self.send_sems.at[small], recv_sem=self.recv_sems.at[sem],
            device_id=self.device(dc=1), device_id_type=MESH)

    def wait(self, group):
        self.waiter(group.tiles, 0, group.sem).wait_recv()

    def drain(self):
        for small, tiles in enumerate(self.sent):
            self.waiter(tiles, small, 0).wait_send()

    @staticmethod
    def at(region):
        r, n, c, w = region
        return (pl.ds(r, n), pl.ds(c, w))

    def push(self, group, region, plane, **to):
        rs, cs = self.at(region)
        self.copy(group, region[1] * region[3] // 1024, self.acc.at[rs, cs], self.got.at[plane, rs, cs], **to)

    def push_z(self, group, region, d):
        self.push(group, region, FROM_Z[d], dz=d)

    def push_y(self, group, region, d):
        self.push(group, region, FROM_Y[d], dy=d)

    def pass_on(self, group, region, **to):
        rs, cs = self.at(region)
        self.copy(group, region[1] * region[3] // 1024, self.full.at[rs, cs], self.full.at[rs, cs], **to)

    def add(self, region, planes):
        rs, cs = self.at(region)
        total = self.acc[rs, cs]
        for p in planes:
            total = total + self.got[p, rs, cs]
        self.acc[rs, cs] = total

    def finish(self, region):
        rs, cs = self.at(region)
        pseudo = self.acc[rs, cs] / REPLICAS
        self.full[rs, cs] = pseudo
        self.squares.append(sum(pseudo[:, i:i + 128] * pseudo[:, i:i + 128] for i in range(0, region[3], 128)))

    def finish_rows(self, region, mine):
        rs, cs = self.at(region)
        even = self.acc[rs, cs] + self.got[FROM_Y[2], rs, cs]
        odd = self.got[FROM_Y[1], rs, cs] + self.got[FROM_Y[-1], rs, cs]
        self.full[rs, cs] = (even + odd) / REPLICAS
        rs, cs = self.at(mine)
        pseudo = self.full[rs, cs]
        self.squares.append(sum(pseudo[:, i:i + 128] * pseudo[:, i:i + 128] for i in range(0, mine[3], 128)))

    def shard(self, d, c, w):
        return (self.rows[d % NZ], 8, c, w)

    def half_shard(self, d, c, w, s):
        h = w // 2
        return self.shard(d, c if s > 0 else c + h, h)

    def push_corners(self, group, c, w, d):
        for q in (2, 1, -1, 0):
            for s in BOTH:
                plane = FROM_Z[s * d] if q == 0 else SPARE[(1 - s) // 2 * 3 + q % NY - 1]
                self.push(group, self.quarter(q, *self.shard(s * d, c, w)), plane, dz=s * d, dy=q)

    def push_rows(self, group, c, w):
        for q in (2, 1, -1):
            self.push_y(group, self.quarter(q, *self.shard(0, c, w)), q)

    def add_corners(self, c, w, d):
        self.add(self.quarter(0, *self.shard(0, c, w)), [FROM_Z[d], FROM_Z[-d], *SPARE, *FROM_Y.values()])

    def scatter_z(self, c, w, depth, merged=False):
        sh = lambda d: self.shard(d, c, w)
        half = lambda d, s: self.half_shard(d, c, w, s)
        g = self.group()
        if merged and depth == 2:
            for s in BOTH:
                self.push_z(g, half(4, s), 2 * s)
            for s in BOTH:
                self.push_z(g, sh(3 * s), s)
            for s in BOTH:
                self.push_z(g, sh(s), s)
            yield g
            self.wait(g)
            g = self.group()
            for s in BOTH:
                self.add(sh(2 * s), [FROM_Z[s]])
                self.add(half(2 * s, s), [FROM_Z[2 * s]])
            self.push_corners(g, c, w, 2)
            self.add(sh(0), [FROM_Z[s] for s in BOTH])
            self.push_rows(g, c, w)
            yield g
            self.wait(g)
            self.add_corners(c, w, 2)
            return
        if depth == 1:
            for d in (4, 3, -3, 2, -2, 1, -1):
                self.push_z(g, sh(d), d)
            yield g
            self.wait(g)
            self.add(sh(0), list(FROM_Z.values()))
            return
        if depth == 4:
            for s in BOTH:
                self.push_z(g, half(4, s), s)
            yield g
            self.wait(g)
            g = self.group()
            for s in BOTH:
                self.add(half(3 * s, s), [FROM_Z[s]])
                self.push_z(g, sh(3 * s), s)
            yield g
            self.wait(g)
            g = self.group()
            for s in BOTH:
                self.add(sh(2 * s), [FROM_Z[s]])
                self.push_z(g, sh(2 * s), s)
        else:
            for s in BOTH:
                self.push_z(g, half(4, s), 2 * s)
            for s in BOTH:
                self.push_z(g, sh(3 * s), s)
            after = self.group()
            if depth == 2:
                for s in BOTH:
                    self.push_z(after, sh(s), s)
            yield g
            self.wait(g)
            for s in BOTH:
                self.add(sh(2 * s), [FROM_Z[s]])
                self.add(half(2 * s, s), [FROM_Z[2 * s]])
                self.push_z(after, sh(2 * s), s if depth == 3 else 2 * s)
            g = after
            if depth == 2:
                yield g
                self.wait(g)
                self.add(sh(0), [FROM_Z[d] for d in (1, -1, 2, -2)])
                return
        if merged:
            last = self.group()
            self.push_rows(last, c, w)
        yield g
        self.wait(g)
        if merged:
            for s in BOTH:
                self.add(sh(s), [FROM_Z[s]])
            self.push_corners(last, c, w, 1)
            yield last
            self.wait(last)
            self.add_corners(c, w, 1)
            return
        g = self.group()
        for s in BOTH:
            self.add(sh(s), [FROM_Z[s]])
            self.push_z(g, sh(s), s)
        yield g
        self.wait(g)
        self.add(sh(0), [FROM_Z[1], FROM_Z[-1]])

    def gather_z(self, c, w, depth, merged=False):
        sh = lambda d: self.shard(d, c, w)
        half = lambda d, s: self.half_shard(d, c, w, s)
        g = self.group()
        if merged:
            mine = self.quarter(0, *sh(0))
            d = 2 if depth == 2 else 1
            for q in (2, 1, -1, 0):
                for s in BOTH:
                    self.pass_on(g, mine, dz=s * d, dy=q)
                if q:
                    self.pass_on(g, mine, dy=q)
            yield g
            self.wait(g)
            g = self.group()
            if depth == 2:
                for s in BOTH:
                    self.pass_on(g, half(-2 * s, s), dz=2 * s)
                for s in BOTH:
                    self.pass_on(g, sh(0), dz=s)
                    self.pass_on(g, sh(-2 * s), dz=s)
                yield g
                self.wait(g)
                return
            for s in BOTH:
                self.pass_on(g, sh(-s), dz=s)
        if depth == 1:
            for d in (4, 3, -3, 2, -2, 1, -1):
                self.pass_on(g, sh(0), dz=d)
            yield g
            self.wait(g)
            return
        if depth == 2 and not merged:
            for s in BOTH:
                self.pass_on(g, sh(0), dz=2 * s)
            last = self.group()
            for s in BOTH:
                self.pass_on(last, sh(0), dz=s)
            yield g
            self.wait(g)
            for s in BOTH:
                self.pass_on(last, half(-2 * s, s), dz=2 * s)
            for s in BOTH:
                self.pass_on(last, sh(-2 * s), dz=s)
            yield last
            self.wait(last)
            return
        if not merged:
            for s in BOTH:
                self.pass_on(g, sh(0), dz=s)
            yield g
            self.wait(g)
            g = self.group()
            for s in BOTH:
                self.pass_on(g, sh(-s), dz=s)
        yield g
        self.wait(g)
        g = self.group()
        if depth == 3:
            for s in BOTH:
                self.pass_on(g, half(-2 * s, s), dz=2 * s)
        for s in BOTH:
            self.pass_on(g, sh(-2 * s), dz=s)
        yield g
        self.wait(g)
        if depth == 4:
            g = self.group()
            for s in BOTH:
                self.pass_on(g, half(-3 * s, s), dz=s)
            yield g
            self.wait(g)

    def quarter(self, d, r, n, c, w):
        return (r, n, pl.multiple_of(c + self.ys[d % NY] * (w // 4), 128), w // 4)

    def half_quarter(self, d, r, n, c, w, s):
        r, n, c, w = self.quarter(d, r, n, c, w)
        if n > 8:
            return (r if s > 0 else r + n // 2, n // 2, c, w)
        return (r, n, c if s > 0 else pl.multiple_of(c + w // 2, 128), w // 2)

    def scatter_y(self, r, n, c, w, depth):
        part = lambda d: self.quarter(d, r, n, c, w)
        half = lambda d, s: self.half_quarter(d, r, n, c, w, s)
        g = self.group()
        if depth == 1:
            for d in (2, 1, -1):
                self.push_y(g, part(d), d)
            yield g
            self.wait(g)
            self.add(part(0), list(FROM_Y.values()))
            return
        for s in BOTH:
            self.push_y(g, half(2, s), s)
        yield g
        self.wait(g)
        g = self.group()
        for s in BOTH:
            self.add(half(s, s), [FROM_Y[s]])
            self.push_y(g, part(s), s)
        yield g
        self.wait(g)
        self.add(part(0), [FROM_Y[s] for s in BOTH])

    def gather_y(self, r, n, c, w, depth):
        part = lambda d: self.quarter(d, r, n, c, w)
        g = self.group()
        for d in (2, 1, -1) if depth == 1 else BOTH:
            self.pass_on(g, part(0), dy=d)
        yield g
        self.wait(g)
        if depth == 2:
            g = self.group()
            for s in BOTH:
                self.pass_on(g, self.half_quarter(-s, r, n, c, w, s), dy=s)
            yield g
            self.wait(g)

    def flow(self, c, w, scatter, scatter_z, scatter_y, gather, gather_z, gather_y):
        r, n, q, v = self.shard(0, *self.quarter(0, 0, 8, c, w)[2:])
        if scatter == "zy":
            yield from self.scatter_z(c, w, scatter_z, scatter_y == 0)
            if scatter_y == 3:
                g = self.group()
                for d in (2, 1, -1):
                    self.push_y(g, (r, n, c, w), d)
                yield g
                self.wait(g)
            elif scatter_y:
                yield from self.scatter_y(r, n, c, w, scatter_y)
        else:
            yield from self.scatter_y(0, ROWS, c, w, scatter_y)
            yield from self.scatter_z(q, v, scatter_z)
        if scatter_y == 3:
            self.finish_rows((r, n, c, w), (r, n, q, v))
        else:
            self.finish((r, n, q, v))
        if gather == "yz":
            if gather_y in (1, 2):
                yield from self.gather_y(r, n, c, w, gather_y)
            yield from self.gather_z(c, w, gather_z, gather_y == 0)
        else:
            yield from self.gather_z(q, v, gather_z)
            yield from self.gather_y(0, ROWS, c, w, gather_y)

    def clip(self, factor, sums, parts):
        while len(self.squares) < len(FLOWS):
            yield None
        total = sum(self.squares)
        n = 0
        for i, stage in enumerate(STAGES):
            sums[i] = total
            g = self.group()
            for j, d in enumerate(stage):
                self.copy(g, 1, sums.at[i], parts.at[n + j], small=1, **d)
            yield g
            self.wait(g)
            total = total + sum(parts[n + j] for j in range(len(stage)))
            n += len(stage)
        mean = jnp.full((8, 128), jnp.sum(total)) / ENTRIES
        factor[...] = jnp.minimum(1.0, 0.5 / jnp.sqrt(mean + 1e-6))


def exchange(outer_hbm, inner_hbm, momentum_hbm, full, factor, outer, inner, momentum, acc, got, sums, parts, send_sems, recv_sems, load_sems):
    ar = AllReduce(acc, got, full, send_sems, recv_sems)
    barrier = pltpu.get_barrier_semaphore()
    loads = []
    for i, (c, w, *_) in enumerate(FLOWS):
        cs = pl.ds(c, w)
        for j, (src, dst) in enumerate(((outer_hbm, outer), (inner_hbm, inner))):
            loads.append(pltpu.make_async_copy(src.at[:, cs], dst.at[:, cs], load_sems.at[2 * i + j]))
    last_load = pltpu.make_async_copy(momentum_hbm, momentum, load_sems.at[len(loads)])
    starts = list(dict.fromkeys(i for i in ORDER if i < len(FLOWS)))
    for p in PEERS:
        pl.semaphore_signal(barrier, inc=1, device_id=ar.device(**p), device_id_type=MESH)
    for i in starts:
        loads[2 * i].start()
        loads[2 * i + 1].start()

    def flow(i, c, w, *plan):
        loads[2 * i].wait()
        loads[2 * i + 1].wait()
        late = plan[0] == "yz" and plan[2] == 2
        parts_of = [ar.quarter(d, 0, ROWS, c, w)[2:] for d in (2, 1, 3, 0)] if late else [(c, w)]

        def differ(first, width):
            cs = pl.ds(first, width)
            acc[:, cs] = outer[:, cs] - inner[:, cs].astype(jnp.float32)

        differ(*parts_of[0])
        if i == starts[0]:
            pl.semaphore_wait(barrier, len(PEERS))
        steps = ar.flow(c, w, *plan)
        waits = next(steps)
        for part in parts_of[1:]:
            differ(*part)
        yield waits
        yield from steps

    flows = [flow(i, *f) for i, f in enumerate(FLOWS)] + [ar.clip(factor, sums, parts)]
    for n, i in enumerate(ORDER):
        next(flows[i], None)
        if n == 2 * len(FLOWS):
            last_load.start()
    assert all(next(g, flows) is flows for g in flows)
    ar.drain()
    last_load.wait()


def all_reduce(outer_param, inner, momentum):
    array = pltpu.VMEM((ROWS, COLS), jnp.float32)
    operands = [pltpu.with_memory_space_constraint(a, pltpu.HBM) for a in (outer_param, inner, momentum)]
    return pl.pallas_call(
        exchange,
        out_shape=(array, pltpu.VMEM((8, 128), jnp.float32), array, pltpu.VMEM((ROWS, COLS), jnp.bfloat16), array),
        in_specs=[pl.BlockSpec(memory_space=pl.ANY)] * 3,
        out_specs=(pl.BlockSpec(memory_space=pltpu.VMEM),) * 5,
        scratch_shapes=[
            pltpu.VMEM((ROWS, COLS), jnp.float32),
            pltpu.VMEM((PLANES, ROWS, COLS), jnp.float32),
            pltpu.VMEM((len(STAGES), 8, 128), jnp.float32),
            pltpu.VMEM((len(PEERS), 8, 128), jnp.float32),
            pltpu.SemaphoreType.DMA((2,)),
            pltpu.SemaphoreType.DMA((MAX_GROUPS,)),
            pltpu.SemaphoreType.DMA((2 * len(FLOWS) + 1,)),
        ],
        compiler_params=pltpu.CompilerParams(collective_id=0, has_side_effects=True, vmem_limit_bytes=32 * 2**20),
    )(*operands)


BLOCK = (16, 4096)
STRIP = 512


def update(pseudo, factor, outer, inner, momentum, new_outer_hbm, new_momentum_hbm, merged_hbm, new_outer, new_momentum, merged, sems):
    f = jnp.broadcast_to(factor[0:1, 0:1], (BLOCK[0], STRIP))
    stores = []
    for r in range(0, ROWS, BLOCK[0]):
        for c in range(0, COLS, BLOCK[1]):
            rs = pl.ds(r, BLOCK[0])

            @pl.loop(c, c + BLOCK[1], step=STRIP)
            def _(i):
                cs = pl.ds(pl.multiple_of(i, STRIP), STRIP)
                grad = f * pseudo[rs, cs]
                m = 0.9 * momentum[rs, cs] + grad
                o = outer[rs, cs] - 0.7 * (grad + 0.9 * m)
                new_momentum[rs, cs] = m
                new_outer[rs, cs] = o
                merged[rs, cs] = (0.5 * inner[rs, cs].astype(jnp.float32) + 0.5 * o).astype(jnp.bfloat16)

            cs = pl.ds(c, BLOCK[1])
            for src, dst in ((new_outer, new_outer_hbm), (new_momentum, new_momentum_hbm), (merged, merged_hbm)):
                stores.append(pltpu.make_async_copy(src.at[rs, cs], dst.at[rs, cs], sems.at[len(stores)]))
                stores[-1].start()
    for s in stores:
        s.wait()


def outer_update(pseudo, factor, outer, inner, momentum):
    shapes = ((ROWS, COLS), jnp.float32), ((ROWS, COLS), jnp.float32), ((ROWS, COLS), jnp.bfloat16)
    return pl.pallas_call(
        update,
        out_shape=[pltpu.HBM(*s) for s in shapes],
        in_specs=[pl.BlockSpec(memory_space=pltpu.VMEM)] * 5,
        out_specs=[pl.BlockSpec(memory_space=pltpu.HBM)] * 3,
        scratch_shapes=[pltpu.VMEM(*s) for s in shapes] + [pltpu.SemaphoreType.DMA((3 * (ROWS // BLOCK[0]) * (COLS // BLOCK[1]),))],
        compiler_params=pltpu.CompilerParams(vmem_limit_bytes=16 * 2**20),
    )(pseudo, factor, outer, inner, momentum)


def body(outer_param, momentum, inner_weights):
    inner = inner_weights[0]
    new_outer, new_momentum, merged = outer_update(*all_reduce(outer_param, inner, momentum))
    return (new_outer, new_momentum, merged[None])


def solution(mesh):
    in_specs = (P("fsdp", None), P("fsdp", None), P("replica", "fsdp", None))
    out_specs = (P("fsdp", None), P("fsdp", None), P("replica", "fsdp", None))
    return jax.shard_map(body, mesh=mesh, in_specs=in_specs, out_specs=out_specs, check_vma=False)
```
